512 devices in a mesh: img: 32 (over z_hi, y, core), txt: 16 (over z_lo, x).
Axes of the slice: x: 4, y: 8, z: 8 (z_hi: 2, z_lo: 4; z = z_hi * 4 + z_lo), core: 2. Of those that a mesh axis runs over, the one named last changes fastest.
Arguments:
- image_features: bfloat16 [4096, 1536], P('img', 'txt'), may hold values from -6 to 6
- text_features: bfloat16 [4096, 1152], P('img', 'txt'), may hold values from -6 to 6
- image_weight: bfloat16 [1536, 1152], P('txt'), may hold values from -0.15625 to 0.15625
- text_weight: bfloat16 [1152, 1152], P('txt'), may hold values from -0.1875 to 0.1875
- pair_index: int32 [4096], P('img'), may hold values from 0 to 4095, each once
Outputs:
- grad_image_weight: float32 [1536, 1152], P('txt')
- grad_text_weight: float32 [1152, 1152], P('txt')
The draws below stay inside these ranges and needn't reach their ends.
Inputs may be any that keep to these rules, and one draw needn't show every extreme that they name: `pair_index`: every text is the pair of exactly one image.
All inputs are finite; a program needn't handle non-finite values.
Results may differ from the reference program's by a relative error of at most 0.023.
Values may be sent and summed in bfloat16 or wider, within the bound.
No kernel may reach another device: no remote copies, remote signals or barrier semaphores. Data moves between devices by JAX's collectives and lax.ppermute only.
A program may use at most 64 MiB of HBM per device.

```python
import jax
import jax.numpy as jnp
from jax import lax

DV = 1536
DT = 1152
E = 1152
R = 8
B = 4096
N_IMG = 32
N_TXT = 16


def levels(own_key, dims, split, low, top_value):
    gain, own = 1.0, jax.random.fold_in(own_key, 6)
    for position, shards_of in split:
        draws = jnp.exp(jax.random.uniform(jax.random.fold_in(own, position), (shards_of,), jnp.float32, low / len(split), top_value / len(split)))
        gain = gain * jnp.repeat(draws, dims[position] // shards_of).reshape([-1 if axis == position else 1 for axis in range(len(dims))])
    return gain


def gaussian(key, dims, scale, most, shards=(), held_as=jnp.bfloat16):
    array = jax.random.normal(key, dims, jnp.float32) * scale
    if len(shards) > 0:
        array = levels(key, dims, shards, -0.22, 0.18) * array
    return jnp.clip(array, min=-most, max=most).astype(held_as)


def setup_inputs(seed: int = 0) -> dict:
    keys = jax.random.split(jax.random.key(seed), 6)
    return {
        "image_features": gaussian(keys[0], (B, DV), 1.0, 6.0, ((0, 32), (1, 16))),
        "text_features": gaussian(keys[1], (B, DT), 1.0, 6.0, ((0, 32), (1, 16))),
        "image_weight": gaussian(keys[2], (DV, E), DV ** -0.5, 0.15625, ((0, 16),)),
        "text_weight": gaussian(keys[3], (DT, E), DT ** -0.5, 0.1875, ((0, 16),)),
        "pair_index": jax.random.permutation(keys[4], B).astype(jnp.int32),
    }


LOGIT_SCALE = 10.0
LOGIT_BIAS = -5.0
eps = 1e-06

def apply_head(features, weight):
    feature_block = features.shape[1] // N_TXT
    total = jnp.zeros((features.shape[0], weight.shape[1]), jnp.float32)
    for block_index in range(N_TXT):
        lower = block_index * feature_block
        partial_sum = jnp.dot(features[:, lower:lower + feature_block], weight[lower:lower + feature_block], preferred_element_type=jnp.float32)
        total = total + lax.optimization_barrier(partial_sum.astype(jnp.bfloat16)).astype(jnp.float32)
    return total

def normalize(pre_values):
    scale = lax.rsqrt(lax.optimization_barrier(jnp.sum(pre_values * pre_values, -1, keepdims=True)) + eps)
    return (pre_values * scale, scale)

def backnorm(unit, scale, upstream):
    along = lax.optimization_barrier(jnp.sum(unit * upstream, -1, keepdims=True))
    return (upstream - unit * along) * scale

def reference(image_features, text_features, image_weight, text_weight, pair_index):
    block_rows = R * N_TXT
    image_unit, image_scale = normalize(apply_head(image_features, image_weight))
    text_unit, text_scale = normalize(apply_head(text_features, text_weight))
    image_emb = image_unit.astype(jnp.bfloat16)
    text_emb = text_unit.astype(jnp.bfloat16)
    groups = text_emb.reshape(N_IMG, N_TXT, R, E).transpose(1, 0, 2, 3).reshape(N_TXT, N_IMG * R, E).astype(jnp.float32)
    text_ids = jnp.arange(B, dtype=jnp.int32).reshape(N_IMG, N_TXT, R).transpose(1, 0, 2).reshape(N_TXT, N_IMG * R)
    image_blocks = image_emb.reshape(N_IMG, block_rows, E).astype(jnp.float32)
    pair_blocks = pair_index.reshape(N_IMG, block_rows)

    def visit_block(carried, inputs):
        block_emb, block_pairs = inputs
        scores = jnp.einsum('jce,be->jcb', groups, block_emb)
        logits = LOGIT_SCALE * scores + LOGIT_BIAS
        label_sign = jnp.where(text_ids[:, :, None] == block_pairs[None, None, :], 1.0, -1.0).astype(jnp.float32)
        pair_grad = (-label_sign * jax.nn.sigmoid(-label_sign * logits)).astype(jnp.bfloat16)
        pair_grad = lax.optimization_barrier(pair_grad).astype(jnp.float32)
        image_parts = LOGIT_SCALE * jnp.einsum('jcb,jce->jbe', pair_grad, groups)
        text_part = LOGIT_SCALE * jnp.einsum('jcb,be->jce', pair_grad, block_emb)
        return (carried + text_part, lax.optimization_barrier(jnp.sum(image_parts, 0)))
    start = jnp.zeros((N_TXT, N_IMG * R, E), jnp.float32)
    text_total, image_total = lax.scan(visit_block, start, (image_blocks, pair_blocks))
    text_grad = text_total.reshape(N_TXT, N_IMG, R, E).transpose(1, 0, 2, 3).reshape(B, E)
    image_grad = image_total.reshape(B, E)
    image_dpre = backnorm(image_unit, image_scale, image_grad)
    text_dpre = backnorm(text_unit, text_scale, text_grad)
    contract = (((0,), (0,)), ((), ()))
    grad_image_weight = lax.dot_general(image_features.astype(jnp.float32), image_dpre, contract, precision=lax.Precision.HIGHEST, preferred_element_type=jnp.float32)
    grad_text_weight = lax.dot_general(text_features.astype(jnp.float32), text_dpre, contract, precision=lax.Precision.HIGHEST, preferred_element_type=jnp.float32)
    return (grad_image_weight, grad_text_weight)
```

```python
import jax
import jax.numpy as jnp
import numpy as np
from jax import lax
from jax.sharding import Mesh
from jax.sharding import PartitionSpec as P

LOGIT_SCALE = 10.0
LOGIT_BIAS = -5.0
EPS = 1e-06
E = 1152
LANES = 128
WIDE = 2 * E + LANES
AXES = ("zh", "y", "core", "zl", "x")
IMG = ("zh", "y", "core")
ZY = ("zh", "y")
TXT = ("zl", "x")
bf16 = jnp.bfloat16
f32 = jnp.float32


def exchange(value, axis):
    return lax.all_to_all(value, axis, 0, 0, tiled=True)


def head_partials(image_features, text_features, image_weight, text_weight):
    image = jnp.dot(image_features, image_weight, preferred_element_type=f32)
    text = jnp.dot(text_features, text_weight, preferred_element_type=f32)
    return jnp.concatenate([image.astype(bf16), text.astype(bf16)], axis=1)


def split_hi_lo(value):
    hi = value.astype(bf16).astype(f32)
    return hi, value - hi


def unit_rows(partials, own_pairs, copies):
    rows = partials.shape[0] // 16
    total = jnp.sum(partials.astype(f32).reshape(16, rows, 2 * E), axis=0)
    pieces = []
    scales = []
    for tower in range(2):
        pre = total[:, tower * E : (tower + 1) * E]
        scale = lax.rsqrt(jnp.sum(pre * pre, -1, keepdims=True) + EPS)
        pieces.append(pre * scale)
        scales.append(scale)
    lane = lax.broadcasted_iota(jnp.int32, (rows, LANES), 1)
    pair_hi = jnp.floor(own_pairs * (1.0 / 64.0))
    pair_lo = own_pairs - 64.0 * pair_hi
    extra = jnp.zeros((rows, LANES), f32)
    columns = [pair_hi, pair_lo, *split_hi_lo(scales[0]), *split_hi_lo(scales[1])]
    for place, column in enumerate(columns):
        extra = jnp.where(lane == place, column, extra)
    row_block = jnp.concatenate(pieces + [extra], axis=1)
    return jnp.tile(row_block, (copies, 1)).astype(bf16)


def grad_terms(n1, n2_blocks, n1_ids_base, n2_ids_bases, n1_count):
    rows = n1.shape[0]
    info = n1[:, 2 * E :].astype(f32)
    n1_pairs = info[:, 0:1] * 64.0 + info[:, 1:2]
    scales = [info[:, 2:3] + info[:, 3:4], info[:, 4:5] + info[:, 5:6]]
    nt = (((1,), (1,)), ((), ()))
    tn = (((0,), (0,)), ((), ()))
    image_grad = jnp.zeros((rows, E), f32)
    text_grad = jnp.zeros((rows, E), f32)
    image1 = n1[:, :E]
    text1 = n1[:, E : 2 * E]
    for block, base in zip(n2_blocks, n2_ids_bases):
        image2 = block[:, :E]
        text2 = block[:, E : 2 * E]
        count = block.shape[0]
        logits = LOGIT_SCALE * lax.dot_general(image1, text2, nt, preferred_element_type=f32) + LOGIT_BIAS
        ids = (base + lax.broadcasted_iota(jnp.int32, (rows, count), 1)).astype(f32)
        label = jnp.where(ids == n1_pairs, 1.0, 0.0)
        pair_grad = (1.0 / (1.0 + jnp.exp(-logits)) - label).astype(bf16)
        image_grad = image_grad + jnp.dot(pair_grad, text2, preferred_element_type=f32)
        logits = LOGIT_SCALE * lax.dot_general(image2, text1, nt, preferred_element_type=f32) + LOGIT_BIAS
        info2 = block[:, 2 * E :].astype(f32)
        n2_pairs = info2[:, 0:1] * 64.0 + info2[:, 1:2]
        place = lax.broadcasted_iota(jnp.int32, (count, rows), 1)
        ids = (n1_ids_base + (place // 8) * 256 + place % 8).astype(f32)
        label = jnp.where(ids == n2_pairs, 1.0, 0.0)
        pair_grad = (1.0 / (1.0 + jnp.exp(-logits)) - label).astype(bf16)
        text_grad = text_grad + lax.dot_general(pair_grad, image2, tn, preferred_element_type=f32)
    pieces = []
    for unit, grad, scale in ((image1, image_grad, scales[0]), (text1, text_grad, scales[1])):
        unit = unit.astype(f32)
        along = jnp.sum(unit * grad, -1, keepdims=True)
        pieces.append(((grad - unit * along) * (scale * LOGIT_SCALE)).T)
    return jnp.concatenate(pieces, axis=0).astype(bf16)


def summed(parts, copies):
    rows = parts.shape[0] // 16
    total = jnp.sum(parts.astype(f32).reshape(16, rows, LANES), axis=0)
    return jnp.tile(total, (copies, 1)).astype(bf16)


def local(image_features, text_features, image_weight, text_weight, pair_index):
    zy = lax.axis_index(ZY)
    zh = lax.axis_index("zh")
    core = lax.axis_index("core")
    txt = lax.axis_index(TXT)
    block_rows = image_features.shape[0]
    own_rows = block_rows // 16
    image_cols = image_features.shape[1]
    text_cols = text_features.shape[1]

    lanes = jnp.concatenate(
        [
            jnp.pad(image_features, ((0, 0), (0, LANES - image_cols))),
            jnp.pad(text_features, ((0, 0), (0, LANES - text_cols))),
        ],
        axis=1,
    )
    everyone = lax.all_gather(lanes, IMG, axis=0, tiled=True)

    partials = exchange(head_partials(image_features, text_features, image_weight, text_weight), TXT)
    own_pairs = lax.dynamic_slice_in_dim(pair_index, txt * own_rows, own_rows, 0).astype(f32)[:, None]
    repeated = unit_rows(partials, own_pairs, 16)
    block = exchange(repeated, TXT)
    sibling = lax.ppermute(block, "core", [(0, 1), (1, 0)])
    n1 = exchange(repeated, ZY)
    own_base = (zy * 2 + core) * block_rows
    sibling_base = (zy * 2 + 1 - core) * block_rows
    n1_base = core * block_rows + txt * own_rows
    terms = grad_terms(n1, [block, sibling], n1_base, [own_base, sibling_base], own_rows)
    dpre = exchange(summed(exchange(terms, ZY), 16), TXT)

    ordered = everyone.reshape(16, 2, 16, own_rows, 2, LANES)
    ordered = lax.dynamic_index_in_dim(ordered, core, 1, keepdims=False)
    ordered = lax.dynamic_index_in_dim(ordered, zh, 3, keepdims=False)
    ordered = ordered.transpose(1, 0, 2, 3).reshape(16, 16 * own_rows, LANES)
    dpre = dpre.reshape(16, -1, LANES)
    weight_grad = jnp.zeros((dpre.shape[1], LANES), f32)
    for step in range(16):
        weight_grad = weight_grad + jnp.dot(dpre[step], ordered[step], preferred_element_type=f32)
    both = lax.all_gather(weight_grad, "core", axis=0, tiled=False)
    weight_grad = jnp.sum(both, axis=0).astype(bf16)
    whole = exchange(jnp.tile(weight_grad, (16, 1)), ZY).astype(f32)
    return whole[:E, :image_cols].T, whole[E:, :text_cols].T


def solution(mesh):
    fine = Mesh(mesh.devices.reshape(2, 8, 2, 4, 4), AXES)
    in_specs = (P(IMG, TXT), P(IMG, TXT), P(TXT, None), P(TXT, None), P(IMG))
    out_specs = (P(TXT, None), P(TXT, None))
    return jax.shard_map(local, mesh=fine, in_specs=in_specs, out_specs=out_specs, check_vma=False)
```

```python
import jax
import jax.numpy as jnp
import numpy as np
from jax import lax
from jax.sharding import Mesh
from jax.sharding import PartitionSpec as P

LOGIT_SCALE = 10.0
LOGIT_BIAS = -5.0
EPS = 1e-06
E = 1152
LANES = 128
WIDE = 2 * E + LANES
AXES = ("zh", "y", "core", "zl", "x")
IMG = ("zh", "y", "core")
ZY = ("zh", "y")
TXT = ("zl", "x")
bf16 = jnp.bfloat16
f32 = jnp.float32


def exchange(value, axis):
    return lax.all_to_all(value, axis, 0, 0, tiled=True)


def head_partials(image_features, text_features, image_weight, text_weight):
    image = jnp.dot(image_features, image_weight, preferred_element_type=f32)
    text = jnp.dot(text_features, text_weight, preferred_element_type=f32)
    return jnp.concatenate([image.astype(bf16), text.astype(bf16)], axis=1)


def split_hi_lo(value):
    hi = value.astype(bf16).astype(f32)
    return hi, value - hi


def unit_rows(partials, own_pairs, copies):
    rows = partials.shape[0] // 16
    total = jnp.sum(partials.astype(f32).reshape(16, rows, 2 * E), axis=0)
    pieces = []
    scales = []
    for tower in range(2):
        pre = total[:, tower * E : (tower + 1) * E]
        scale = lax.rsqrt(jnp.sum(pre * pre, -1, keepdims=True) + EPS)
        pieces.append(pre * scale)
        scales.append(scale)
    lane = lax.broadcasted_iota(jnp.int32, (rows, LANES), 1)
    pair_hi = jnp.floor(own_pairs * (1.0 / 64.0))
    pair_lo = own_pairs - 64.0 * pair_hi
    extra = jnp.zeros((rows, LANES), f32)
    columns = [pair_hi, pair_lo, *split_hi_lo(scales[0]), *split_hi_lo(scales[1])]
    for place, column in enumerate(columns):
        extra = jnp.where(lane == place, column, extra)
    row_block = jnp.concatenate(pieces + [extra], axis=1)
    return jnp.tile(row_block, (copies, 1)).astype(bf16)


def grad_terms(n1, n2_blocks, n1_ids_base, n2_ids_bases, n1_count):
    rows = n1.shape[0]
    info = n1[:, 2 * E :].astype(f32)
    n1_pairs = info[:, 0:1] * 64.0 + info[:, 1:2]
    scales = [info[:, 2:3] + info[:, 3:4], info[:, 4:5] + info[:, 5:6]]
    nt = (((1,), (1,)), ((), ()))
    tn = (((0,), (0,)), ((), ()))
    image_grad = jnp.zeros((rows, E), f32)
    text_grad = jnp.zeros((rows, E), f32)
    image1 = n1[:, :E]
    text1 = n1[:, E : 2 * E]
    for block, base in zip(n2_blocks, n2_ids_bases):
        image2 = block[:, :E]
        text2 = block[:, E : 2 * E]
        count = block.shape[0]
        logits = LOGIT_SCALE * lax.dot_general(image1, text2, nt, preferred_element_type=f32) + LOGIT_BIAS
        ids = (base + lax.broadcasted_iota(jnp.int32, (rows, count), 1)).astype(f32)
        label = jnp.where(ids == n1_pairs, 1.0, 0.0)
        pair_grad = (1.0 / (1.0 + jnp.exp(-logits)) - label).astype(bf16)
        image_grad = image_grad + jnp.dot(pair_grad, text2, preferred_element_type=f32)
        logits = LOGIT_SCALE * lax.dot_general(image2, text1, nt, preferred_element_type=f32) + LOGIT_BIAS
        info2 = block[:, 2 * E :].astype(f32)
        n2_pairs = info2[:, 0:1] * 64.0 + info2[:, 1:2]
        place = lax.broadcasted_iota(jnp.int32, (count, rows), 1)
        ids = (n1_ids_base + (place // 8) * 256 + place % 8).astype(f32)
        label = jnp.where(ids == n2_pairs, 1.0, 0.0)
        pair_grad = (1.0 / (1.0 + jnp.exp(-logits)) - label).astype(bf16)
        text_grad = text_grad + lax.dot_general(pair_grad, image2, tn, preferred_element_type=f32)
    pieces = []
    for unit, grad, scale in ((image1, image_grad, scales[0]), (text1, text_grad, scales[1])):
        unit = unit.astype(f32)
        along = jnp.sum(unit * grad, -1, keepdims=True)
        pieces.append(((grad - unit * along) * (scale * LOGIT_SCALE)).T)
    return jnp.concatenate(pieces, axis=0).astype(bf16)


def summed(parts, copies):
    rows = parts.shape[0] // 16
    total = jnp.sum(parts.astype(f32).reshape(16, rows, LANES), axis=0)
    return jnp.tile(total, (copies, 1)).astype(bf16)


def local(image_features, text_features, image_weight, text_weight, pair_index):
    zy = lax.axis_index(ZY)
    core = lax.axis_index("core")
    txt = lax.axis_index(TXT)
    block_rows = image_features.shape[0]
    own_rows = block_rows // 16
    image_cols = image_features.shape[1]
    text_cols = text_features.shape[1]

    def by_own_rows(features, cols):
        padded = jnp.pad(features, ((0, 0), (0, LANES - cols)))
        return padded.reshape(16, own_rows, LANES).transpose(1, 0, 2).reshape(own_rows, 16 * LANES)

    image_rows = by_own_rows(image_features, image_cols)
    text_rows = by_own_rows(text_features, text_cols)
    feature_rows = jnp.concatenate([jnp.tile(image_rows, (8, 1)), jnp.tile(text_rows, (8, 1))], axis=0)

    partials = exchange(head_partials(image_features, text_features, image_weight, text_weight), TXT)
    own_pairs = lax.dynamic_slice_in_dim(pair_index, txt * own_rows, own_rows, 0).astype(f32)[:, None]
    repeated = unit_rows(partials, own_pairs, 16)
    block = exchange(repeated, TXT)
    sibling = lax.ppermute(block, "core", [(0, 1), (1, 0)])
    received = exchange(jnp.concatenate([repeated, feature_rows], axis=1), ZY)
    n1 = received[:, :WIDE]
    own_base = (zy * 2 + core) * block_rows
    sibling_base = (zy * 2 + 1 - core) * block_rows
    n1_base = core * block_rows + txt * own_rows
    terms = grad_terms(n1, [block, sibling], n1_base, [own_base, sibling_base], own_rows)
    dpre = exchange(summed(exchange(terms, ZY), 16), TXT)

    dpre = dpre.reshape(16, -1, LANES)
    weight_grad = jnp.zeros((dpre.shape[1], LANES), f32)
    for step in range(16):
        ordered = received[:, WIDE + step * LANES : WIDE + (step + 1) * LANES]
        weight_grad = weight_grad + jnp.dot(dpre[step], ordered, preferred_element_type=f32)
    both = lax.all_gather(weight_grad, "core", axis=0, tiled=False)
    weight_grad = jnp.sum(both, axis=0).astype(bf16)
    whole = exchange(jnp.tile(weight_grad, (16, 1)), ZY).astype(f32)
    return whole[:E, :image_cols].T, whole[E:, :text_cols].T


def solution(mesh):
    fine = Mesh(mesh.devices.reshape(2, 8, 2, 4, 4), AXES)
    in_specs = (P(IMG, TXT), P(IMG, TXT), P(TXT, None), P(TXT, None), P(IMG))
    out_specs = (P(TXT, None), P(TXT, None))
    return jax.shard_map(local, mesh=fine, in_specs=in_specs, out_specs=out_specs, check_vma=False)
```

```python
import jax
import jax.numpy as jnp
from jax import lax
from jax.sharding import Mesh
from jax.sharding import PartitionSpec as P

LOGIT_SCALE = 10.0
LOGIT_BIAS = -5.0
EPS = 1e-06
E = 1152
LANES = 128
AXES = ("zh", "y", "core", "zl", "x")
IMG = ("zh", "y", "core")
ZY = ("zh", "y")
TXT = ("zl", "x")
bf16 = jnp.bfloat16
f32 = jnp.float32


def exchange(value, axis):
    return lax.all_to_all(value, axis, 0, 0, tiled=True)


def swap(value, axis):
    return lax.ppermute(value, axis, [(0, 1), (1, 0)])


def head_partials(image_features, text_features, image_weight, text_weight):
    image = jnp.dot(image_features, image_weight, preferred_element_type=f32)
    text = jnp.dot(text_features, text_weight, preferred_element_type=f32)
    return jnp.concatenate([image.astype(bf16), text.astype(bf16)], axis=1)


def columns_in_lanes(columns, rows):
    lane = lax.broadcasted_iota(jnp.int32, (rows, LANES), 1)
    lanes = jnp.zeros((rows, LANES), f32)
    for place, column in enumerate(columns):
        lanes = jnp.where(lane == place, column, lanes)
    return lanes


def key_digits(key):
    hi = jnp.floor(key * (1.0 / 64.0))
    return [hi, key - 64.0 * hi]


def hi_lo(value):
    hi = value.astype(bf16).astype(f32)
    return [hi, value - hi]


def unit_rows(partials, pairs, ids):
    rows = partials.shape[0] // 16
    total = jnp.sum(partials.astype(f32).reshape(16, rows, 2 * E), axis=0)
    first, second = [], []
    for tower, (key1, key2) in enumerate(((pairs, pairs), (ids, ids))):
        pre = total[:, tower * E : (tower + 1) * E]
        scale = lax.rsqrt(jnp.sum(pre * pre, -1, keepdims=True) + EPS)
        unit = pre * scale
        extra1 = columns_in_lanes(key_digits(key1) + hi_lo(scale), rows)
        extra2 = columns_in_lanes(key_digits(key2), rows)
        first.append(jnp.concatenate([unit, extra1], axis=1).astype(bf16))
        second.append(jnp.concatenate([unit, extra2], axis=1).astype(bf16))
    return first, second


def grad_terms(n1, n2_blocks):
    rows = n1.shape[0]
    info = n1[:, E : E + LANES].astype(f32)
    key1 = info[:, 0:1] * 64.0 + info[:, 1:2]
    scale = info[:, 2:3] + info[:, 3:4]
    unit = n1[:, :E]
    grad = jnp.zeros((rows, E), f32)
    for block in n2_blocks:
        other = block[:, :E]
        info2 = block[:, E:].astype(f32).T
        key2 = info2[0:1] * 64.0 + info2[1:2]
        scores = lax.dot_general(unit, other, (((1,), (1,)), ((), ())), preferred_element_type=f32)
        logits = LOGIT_SCALE * scores + LOGIT_BIAS
        label = jnp.where(key1 == key2, 1.0, 0.0)
        pair_grad = (1.0 / (1.0 + jnp.exp(-logits)) - label).astype(bf16)
        grad = grad + jnp.dot(pair_grad, other, preferred_element_type=f32)
    unit = unit.astype(f32)
    along = jnp.sum(unit * grad, -1, keepdims=True)
    return ((grad - unit * along) * (scale * LOGIT_SCALE)).T.astype(bf16)


def local(image_features, text_features, image_weight, text_weight, pair_index):
    zh = lax.axis_index("zh")
    img = lax.axis_index(IMG)
    txt = lax.axis_index(TXT)
    block_rows = image_features.shape[0]
    own_rows = block_rows // 16
    image_cols = image_features.shape[1]
    text_cols = text_features.shape[1]

    def by_own_rows(features, cols):
        padded = jnp.pad(features, ((0, 0), (0, LANES - cols)))
        return padded.reshape(16, own_rows, LANES).transpose(1, 0, 2).reshape(own_rows, 16 * LANES)

    def pick(one, two):
        return jnp.where(zh == 0, one, two)

    features = [by_own_rows(image_features, image_cols), by_own_rows(text_features, text_cols)]
    partials = exchange(head_partials(image_features, text_features, image_weight, text_weight), TXT)
    pairs = lax.dynamic_slice_in_dim(pair_index, txt * own_rows, own_rows, 0).astype(f32)[:, None]
    ids = (img * block_rows + txt * own_rows + jnp.arange(own_rows)).astype(f32)[:, None]
    first, second = unit_rows(partials, pairs, ids)

    n1_own, n1_given = pick(*first), pick(*first[::-1])
    n2_own, n2_given = pick(*second[::-1]), pick(*second)
    x_own, x_given = pick(*features), pick(*features[::-1])
    given = swap(jnp.concatenate([n1_given, x_given, n2_given], axis=1), "zh")
    width = n1_own.shape[1] + x_own.shape[1]
    n1_own = jnp.concatenate([n1_own, x_own], axis=1)
    n1_own = jnp.concatenate([pick(n1_own, given[:, :width]), pick(given[:, :width], n1_own)], axis=0)
    n2_own = jnp.concatenate([pick(n2_own, given[:, width:]), pick(given[:, width:], n2_own)], axis=0)

    column = exchange(jnp.tile(n2_own, (4, 1)), "zl")
    column, n1_own = lax.optimization_barrier((column, n1_own))
    block = [column] + [lax.ppermute(column, "x", [(i, i ^ step) for i in range(4)]) for step in (1, 2, 3)]
    block = jnp.concatenate(block, axis=0)
    n1 = exchange(jnp.tile(n1_own, (8, 1)), "y")
    terms = grad_terms(n1, [block, swap(block, "core")])

    chunk = E // 8
    dpre = jnp.sum(exchange(terms, "y").astype(f32).reshape(8, chunk, -1), axis=0).astype(bf16)
    dpre = exchange(jnp.tile(dpre, (16, 1)), TXT).reshape(16, chunk, -1)
    weight_grad = jnp.zeros((chunk, LANES), f32)
    for step in range(16):
        rows = n1[:, E + LANES * (step + 1) : E + LANES * (step + 2)]
        weight_grad = weight_grad + jnp.dot(dpre[step], rows, preferred_element_type=f32)
    both = lax.all_gather(weight_grad, "core", axis=0, tiled=False)
    weight_grad = jnp.sum(both, axis=0).astype(bf16)
    whole = exchange(jnp.tile(weight_grad, (16, 1)), ZY).astype(f32)
    return whole[:E, :image_cols].T, whole[E:, :text_cols].T


def solution(mesh):
    fine = Mesh(mesh.devices.reshape(2, 8, 2, 4, 4), AXES)
    in_specs = (P(IMG, TXT), P(IMG, TXT), P(TXT, None), P(TXT, None), P(IMG))
    out_specs = (P(TXT, None), P(TXT, None))
    return jax.shard_map(local, mesh=fine, in_specs=in_specs, out_specs=out_specs, check_vma=False)
```

```python
import jax
import jax.numpy as jnp
from jax import lax
from jax.sharding import Mesh
from jax.sharding import PartitionSpec as P

LOGIT_SCALE = 10.0
LOGIT_BIAS = -5.0
EPS = 1e-06
E = 1152
LANES = 128
AXES = ("zh", "y", "core", "zl", "x")
IMG = ("zh", "y", "core")
ZY = ("zh", "y")
TXT = ("zl", "x")
bf16 = jnp.bfloat16
f32 = jnp.float32


def exchange(value, axis):
    return lax.all_to_all(value, axis, 0, 0, tiled=True)


def swap(value, axis):
    return lax.ppermute(value, axis, [(0, 1), (1, 0)])


def head_partials(image_features, text_features, image_weight, text_weight):
    image = jnp.dot(image_features, image_weight, preferred_element_type=f32)
    text = jnp.dot(text_features, text_weight, preferred_element_type=f32)
    return jnp.concatenate([image.astype(bf16), text.astype(bf16)], axis=1)


def columns_in_lanes(columns, rows):
    lane = lax.broadcasted_iota(jnp.int32, (rows, LANES), 1)
    lanes = jnp.zeros((rows, LANES), f32)
    for place, column in enumerate(columns):
        lanes = jnp.where(lane == place, column, lanes)
    return lanes


def key_digits(key):
    hi = jnp.floor(key * (1.0 / 64.0))
    return [hi, key - 64.0 * hi]


def hi_lo(value):
    hi = value.astype(bf16).astype(f32)
    return [hi, value - hi]


def unit_rows(partials, pairs, ids):
    rows = partials.shape[0] // 16
    total = jnp.sum(partials.astype(f32).reshape(16, rows, 2 * E), axis=0)
    first, second = [], []
    for tower, (key1, key2) in enumerate(((pairs, pairs), (ids, ids))):
        pre = total[:, tower * E : (tower + 1) * E]
        scale = lax.rsqrt(jnp.sum(pre * pre, -1, keepdims=True) + EPS)
        unit = pre * scale
        extra1 = columns_in_lanes(key_digits(key1) + hi_lo(scale), rows)
        extra2 = columns_in_lanes(key_digits(key2), rows)
        first.append(jnp.concatenate([unit, extra1], axis=1).astype(bf16))
        second.append(jnp.concatenate([unit, extra2], axis=1).astype(bf16))
    return first, second


def grad_terms(n1, n2_blocks):
    rows = n1.shape[0]
    info = n1[:, E : E + LANES].astype(f32)
    key1 = info[:, 0:1] * 64.0 + info[:, 1:2]
    scale = info[:, 2:3] + info[:, 3:4]
    unit = n1[:, :E]
    grad = jnp.zeros((rows, E), f32)
    for block in n2_blocks:
        other = block[:, :E]
        info2 = block[:, E:].astype(f32).T
        key2 = info2[0:1] * 64.0 + info2[1:2]
        scores = lax.dot_general(unit, other, (((1,), (1,)), ((), ())), preferred_element_type=f32)
        logits = LOGIT_SCALE * scores + LOGIT_BIAS
        label = jnp.where(key1 == key2, 1.0, 0.0)
        pair_grad = (1.0 / (1.0 + jnp.exp(-logits)) - label).astype(bf16)
        grad = grad + jnp.dot(pair_grad, other, preferred_element_type=f32)
    unit = unit.astype(f32)
    along = jnp.sum(unit * grad, -1, keepdims=True)
    return ((grad - unit * along) * (scale * LOGIT_SCALE)).T.astype(bf16)


def local(image_features, text_features, image_weight, text_weight, pair_index):
    zh = lax.axis_index("zh")
    img = lax.axis_index(IMG)
    txt = lax.axis_index(TXT)
    block_rows = image_features.shape[0]
    own_rows = block_rows // 16
    image_cols = image_features.shape[1]
    text_cols = text_features.shape[1]

    def by_own_rows(features, cols):
        padded = jnp.pad(features, ((0, 0), (0, LANES - cols)))
        return padded.reshape(16, own_rows, LANES).transpose(1, 0, 2).reshape(own_rows, 16 * LANES)

    def pick(one, two):
        return jnp.where(zh == 0, one, two)

    features = [by_own_rows(image_features, image_cols), by_own_rows(text_features, text_cols)]
    partials = exchange(head_partials(image_features, text_features, image_weight, text_weight), TXT)
    pairs = lax.dynamic_slice_in_dim(pair_index, txt * own_rows, own_rows, 0).astype(f32)[:, None]
    ids = (img * block_rows + txt * own_rows + jnp.arange(own_rows)).astype(f32)[:, None]
    first, second = unit_rows(partials, pairs, ids)

    n1_own, n1_given = pick(*first), pick(*first[::-1])
    x_own, x_given = pick(*features), pick(*features[::-1])
    n1_own = jnp.concatenate([n1_own, x_own], axis=1)
    given = swap(jnp.concatenate([n1_given, x_given], axis=1), "zh")
    n1_own = jnp.concatenate([pick(n1_own, given), pick(given, n1_own)], axis=0)

    column = exchange(jnp.concatenate([jnp.tile(second[1], (4, 1)), jnp.tile(second[0], (4, 1))], axis=0), ("zh", "zl"))
    column, n1_own = lax.optimization_barrier((column, n1_own))
    block = [column] + [lax.ppermute(column, "x", [(i, i ^ step) for i in range(4)]) for step in (1, 2, 3)]
    block = jnp.concatenate(block, axis=0)
    n1 = exchange(jnp.tile(n1_own, (8, 1)), "y")
    block, n1 = lax.optimization_barrier((block, n1))
    terms = grad_terms(n1, [block, swap(block, "core")])

    chunk = E // 8
    dpre = jnp.sum(exchange(terms, "y").astype(f32).reshape(8, chunk, -1), axis=0).astype(bf16)
    dpre = exchange(jnp.tile(dpre, (16, 1)), TXT).reshape(16, chunk, -1)
    weight_grad = jnp.zeros((chunk, LANES), f32)
    for step in range(16):
        rows = n1[:, E + LANES * (step + 1) : E + LANES * (step + 2)]
        weight_grad = weight_grad + jnp.dot(dpre[step], rows, preferred_element_type=f32)
    both = lax.all_gather(weight_grad, "core", axis=0, tiled=False)
    half = chunk // 2
    weight_grad = lax.dynamic_slice_in_dim(jnp.sum(both, axis=0), lax.axis_index("core") * half, half, 0).astype(bf16)
    halves = exchange(jnp.tile(weight_grad, (16, 1)), ZY)
    whole = lax.all_gather(halves, "core", axis=0, tiled=False).reshape(2, 16, half, LANES).astype(f32)
    whole = whole.transpose(1, 0, 2, 3).reshape(2 * E, LANES)
    return whole[:E, :image_cols].T, whole[E:, :text_cols].T


def solution(mesh):
    fine = Mesh(mesh.devices.reshape(2, 8, 2, 4, 4), AXES)
    in_specs = (P(IMG, TXT), P(IMG, TXT), P(TXT, None), P(TXT, None), P(IMG))
    out_specs = (P(TXT, None), P(TXT, None))
    return jax.shard_map(local, mesh=fine, in_specs=in_specs, out_specs=out_specs, check_vma=False)
```

```python
import jax
import jax.numpy as jnp
from jax import lax
from jax.experimental import pallas as pl
from jax.sharding import Mesh
from jax.sharding import PartitionSpec as P

LOGIT_SCALE = 10.0
LOGIT_BIAS = -5.0
EPS = 1e-06
E = 1152
LANES = 128
AXES = ("zh", "y", "core", "zl", "x")
IMG = ("zh", "y", "core")
ZY = ("zh", "y")
TXT = ("zl", "x")
bf16 = jnp.bfloat16
f32 = jnp.float32


def exchange(value, axis):
    return lax.all_to_all(value, axis, 0, 0, tiled=True)


def swap(value, axis):
    return lax.ppermute(value, axis, [(0, 1), (1, 0)])


def head_kernel(image_ref, text_ref, image_weight_ref, text_weight_ref, out_ref):
    tn = (((0,), (0,)), ((), ()))
    for tower, (features, weight) in enumerate(((image_ref, image_weight_ref), (text_ref, text_weight_ref))):
        rows = features[...]
        out_ref[:, tower * E : (tower + 1) * E] = lax.dot_general(
            rows, weight[...], tn, preferred_element_type=f32
        ).astype(bf16)
        square = (rows.shape[0], LANES)
        same = lax.broadcasted_iota(jnp.int32, square, 0) == lax.broadcasted_iota(jnp.int32, square, 1)
        place = jnp.where(same, 1.0, 0.0).astype(bf16)
        out_ref[:, 2 * E + tower * LANES : 2 * E + (tower + 1) * LANES] = lax.dot_general(
            rows, place, tn, preferred_element_type=f32
        ).astype(bf16)


def head_partials(image_features, text_features, image_weight, text_weight):
    return pl.pallas_call(
        head_kernel,
        out_shape=jax.ShapeDtypeStruct((image_features.shape[0], 2 * E + 2 * LANES), bf16),
        name="head_partials",
    )(image_features.T, text_features.T, image_weight, text_weight)


def columns_in_lanes(columns, rows):
    lane = lax.broadcasted_iota(jnp.int32, (rows, LANES), 1)
    lanes = jnp.zeros((rows, LANES), f32)
    for place, column in enumerate(columns):
        lanes = jnp.where(lane == place, column, lanes)
    return lanes


def key_digits(key):
    hi = jnp.floor(key * (1.0 / 64.0))
    return [hi, key - 64.0 * hi]


def hi_lo(value):
    hi = value.astype(bf16).astype(f32)
    return [hi, value - hi]


def unit_rows(partials, pairs, ids):
    rows = partials.shape[0] // 16
    total = jnp.sum(partials[:, : 2 * E].astype(f32).reshape(16, rows, 2 * E), axis=0)
    first, second = [], []
    for tower, (key1, key2) in enumerate(((pairs, pairs), (ids, ids))):
        pre = total[:, tower * E : (tower + 1) * E]
        scale = lax.rsqrt(jnp.sum(pre * pre, -1, keepdims=True) + EPS)
        unit = pre * scale
        extra1 = columns_in_lanes(key_digits(key1) + hi_lo(scale), rows)
        extra2 = columns_in_lanes(key_digits(key2), rows)
        first.append(jnp.concatenate([unit, extra1], axis=1).astype(bf16))
        second.append(jnp.concatenate([unit, extra2], axis=1).astype(bf16))
    return first, second


def grad_terms(n1, n2_blocks):
    rows = n1.shape[0]
    info = n1[:, E : E + LANES].astype(f32)
    key1 = info[:, 0:1] * 64.0 + info[:, 1:2]
    scale = info[:, 2:3] + info[:, 3:4]
    unit = n1[:, :E]
    grad = jnp.zeros((rows, E), f32)
    for block in n2_blocks:
        other = block[:, :E]
        info2 = block[:, E:].astype(f32).T
        key2 = info2[0:1] * 64.0 + info2[1:2]
        scores = lax.dot_general(unit, other, (((1,), (1,)), ((), ())), preferred_element_type=f32)
        logits = LOGIT_SCALE * scores + LOGIT_BIAS
        label = jnp.where(key1 == key2, 1.0, 0.0)
        pair_grad = (1.0 / (1.0 + jnp.exp(-logits)) - label).astype(bf16)
        grad = grad + jnp.dot(pair_grad, other, preferred_element_type=f32)
    unit = unit.astype(f32)
    along = jnp.sum(unit * grad, -1, keepdims=True)
    return ((grad - unit * along) * (scale * LOGIT_SCALE)).T.astype(bf16)


def local(image_features, text_features, image_weight, text_weight, pair_index):
    zh = lax.axis_index("zh")
    img = lax.axis_index(IMG)
    txt = lax.axis_index(TXT)
    block_rows = image_features.shape[0]
    own_rows = block_rows // 16
    image_cols = image_features.shape[1]
    text_cols = text_features.shape[1]

    def pick(one, two):
        return jnp.where(zh == 0, one, two)

    partials = exchange(head_partials(image_features, text_features, image_weight, text_weight), TXT)

    def all_features(tower):
        part = partials[:, 2 * E + tower * LANES : 2 * E + (tower + 1) * LANES]
        return part.reshape(16, own_rows, LANES).transpose(1, 0, 2).reshape(own_rows, 16 * LANES)

    features = [all_features(0), all_features(1)]
    pairs = lax.dynamic_slice_in_dim(pair_index, txt * own_rows, own_rows, 0).astype(f32)[:, None]
    ids = (img * block_rows + txt * own_rows + jnp.arange(own_rows)).astype(f32)[:, None]
    first, second = unit_rows(partials, pairs, ids)

    n1_own, n1_given = pick(*first), pick(*first[::-1])
    x_own, x_given = pick(*features), pick(*features[::-1])
    n1_own = jnp.concatenate([n1_own, x_own], axis=1)
    given = swap(jnp.concatenate([n1_given, x_given], axis=1), "zh")
    n1_own = jnp.concatenate([pick(n1_own, given), pick(given, n1_own)], axis=0)

    column = exchange(jnp.concatenate([jnp.tile(second[1], (4, 1)), jnp.tile(second[0], (4, 1))], axis=0), ("zh", "zl"))
    block = [column] + [lax.ppermute(column, "x", [(i, i ^ step) for i in range(4)]) for step in (1, 2, 3)]
    block = jnp.concatenate(block, axis=0)
    n1 = exchange(jnp.tile(n1_own, (8, 1)), "y")
    terms = grad_terms(n1, [block, swap(block, "core")])

    features = n1[:, E + LANES :]
    terms, features = lax.optimization_barrier((terms, features))
    other_features = swap(features, "core")
    chunk = E // 8
    half = chunk // 2
    core = lax.axis_index("core")
    parts, other_features = lax.optimization_barrier((exchange(terms, "y"), other_features))
    dpre = jnp.sum(parts.astype(f32).reshape(8, chunk, -1), axis=0).astype(bf16)
    kept = jnp.where(core == 0, dpre[:half], dpre[half:])
    given = swap(jnp.where(core == 0, dpre[half:], dpre[:half]), "core")
    weight_grad = jnp.dot(kept, features, preferred_element_type=f32)
    weight_grad = weight_grad + jnp.dot(given, other_features, preferred_element_type=f32)
    parts = weight_grad.astype(bf16).reshape(half, 16, LANES).transpose(1, 0, 2).reshape(16 * half, LANES)
    parts = exchange(parts, TXT).astype(f32).reshape(16, half, LANES)
    weight_grad = jnp.sum(parts, axis=0).astype(bf16)
    halves = exchange(jnp.tile(weight_grad, (16, 1)), ZY)
    whole = lax.all_gather(halves, "core", axis=0, tiled=False).reshape(2, 16, half, LANES).astype(f32)
    whole = whole.transpose(1, 0, 2, 3).reshape(2 * E, LANES)
    return whole[:E, :image_cols].T, whole[E:, :text_cols].T


def solution(mesh):
    fine = Mesh(mesh.devices.reshape(2, 8, 2, 4, 4), AXES)
    in_specs = (P(IMG, TXT), P(IMG, TXT), P(TXT, None), P(TXT, None), P(IMG))
    out_specs = (P(TXT, None), P(TXT, None))
    return jax.shard_map(local, mesh=fine, in_specs=in_specs, out_specs=out_specs, check_vma=False)
```

```python
import jax
import jax.numpy as jnp
from jax import lax
from jax.experimental import pallas as pl
from jax.sharding import Mesh
from jax.sharding import PartitionSpec as P

LOGIT_SCALE = 10.0
LOGIT_BIAS = -5.0
EPS = 1e-06
E = 1152
LANES = 128
AXES = ("zh", "y", "core", "zl", "x")
IMG = ("zh", "y", "core")
ZY = ("zh", "y")
TXT = ("zl", "x")
bf16 = jnp.bfloat16
f32 = jnp.float32


def exchange(value, axis):
    return lax.all_to_all(value, axis, 0, 0, tiled=True)


def swap(value, axis):
    return lax.ppermute(value, axis, [(0, 1), (1, 0)])


def head_kernel(image_ref, text_ref, image_weight_ref, text_weight_ref, out_ref):
    tn = (((0,), (0,)), ((), ()))
    for tower, (features, weight) in enumerate(((image_ref, image_weight_ref), (text_ref, text_weight_ref))):
        rows = features[...]
        out_ref[:, tower * E : (tower + 1) * E] = lax.dot_general(
            rows, weight[...], tn, preferred_element_type=f32
        ).astype(bf16)
        square = (rows.shape[0], LANES)
        same = lax.broadcasted_iota(jnp.int32, square, 0) == lax.broadcasted_iota(jnp.int32, square, 1)
        place = jnp.where(same, 1.0, 0.0).astype(bf16)
        out_ref[:, 2 * E + tower * LANES : 2 * E + (tower + 1) * LANES] = lax.dot_general(
            rows, place, tn, preferred_element_type=f32
        ).astype(bf16)


def head_partials(image_features, text_features, image_weight, text_weight):
    return pl.pallas_call(
        head_kernel,
        out_shape=jax.ShapeDtypeStruct((image_features.shape[0], 2 * E + 2 * LANES), bf16),
        name="head_partials",
    )(image_features.T, text_features.T, image_weight, text_weight)


def columns_in_lanes(columns, rows):
    lane = lax.broadcasted_iota(jnp.int32, (rows, LANES), 1)
    lanes = jnp.zeros((rows, LANES), f32)
    for place, column in enumerate(columns):
        lanes = jnp.where(lane == place, column, lanes)
    return lanes


def key_digits(key):
    hi = jnp.floor(key * (1.0 / 64.0))
    return [hi, key - 64.0 * hi]


def hi_lo(value):
    hi = value.astype(bf16).astype(f32)
    return [hi, value - hi]


def unit_rows(partials, pairs, ids):
    rows = partials.shape[0] // 16
    total = jnp.sum(partials[:, : 2 * E].astype(f32).reshape(16, rows, 2 * E), axis=0)
    first, second = [], []
    for tower, (key1, key2) in enumerate(((pairs, pairs), (ids, ids))):
        pre = total[:, tower * E : (tower + 1) * E]
        scale = lax.rsqrt(jnp.sum(pre * pre, -1, keepdims=True) + EPS)
        unit = pre * scale
        extra1 = columns_in_lanes(key_digits(key1) + hi_lo(scale), rows)
        extra2 = columns_in_lanes(key_digits(key2), rows)
        first.append(jnp.concatenate([unit, extra1], axis=1).astype(bf16))
        second.append(jnp.concatenate([unit, extra2], axis=1).astype(bf16))
    return first, second


def grad_terms(n1, n2_blocks):
    rows = n1.shape[0]
    info = n1[:, E : E + LANES].astype(f32)
    key1 = info[:, 0:1] * 64.0 + info[:, 1:2]
    scale = info[:, 2:3] + info[:, 3:4]
    unit = n1[:, :E]
    grad = jnp.zeros((rows, E), f32)
    for block in n2_blocks:
        other = block[:, :E]
        info2 = block[:, E:].astype(f32).T
        key2 = info2[0:1] * 64.0 + info2[1:2]
        scores = lax.dot_general(unit, other, (((1,), (1,)), ((), ())), preferred_element_type=f32)
        logits = LOGIT_SCALE * scores + LOGIT_BIAS
        label = jnp.where(key1 == key2, 1.0, 0.0)
        pair_grad = (1.0 / (1.0 + jnp.exp(-logits)) - label).astype(bf16)
        grad = grad + jnp.dot(pair_grad, other, preferred_element_type=f32)
    unit = unit.astype(f32)
    along = jnp.sum(unit * grad, -1, keepdims=True)
    return ((grad - unit * along) * (scale * LOGIT_SCALE)).T.astype(bf16)


def local(image_features, text_features, image_weight, text_weight, pair_index):
    zh = lax.axis_index("zh")
    img = lax.axis_index(IMG)
    txt = lax.axis_index(TXT)
    block_rows = image_features.shape[0]
    own_rows = block_rows // 16
    image_cols = image_features.shape[1]
    text_cols = text_features.shape[1]

    def pick(one, two):
        return jnp.where(zh == 0, one, two)

    partials = exchange(head_partials(image_features, text_features, image_weight, text_weight), TXT)

    def all_features(tower):
        part = partials[:, 2 * E + tower * LANES : 2 * E + (tower + 1) * LANES]
        return part.reshape(16, own_rows, LANES).transpose(1, 0, 2).reshape(own_rows, 16 * LANES)

    features = [all_features(0), all_features(1)]
    pairs = lax.dynamic_slice_in_dim(pair_index, txt * own_rows, own_rows, 0).astype(f32)[:, None]
    ids = (img * block_rows + txt * own_rows + jnp.arange(own_rows)).astype(f32)[:, None]
    first, second = unit_rows(partials, pairs, ids)

    n1_own, n1_given = pick(*first), pick(*first[::-1])
    x_own, x_given = pick(*features), pick(*features[::-1])
    n1_own = jnp.concatenate([n1_own, x_own], axis=1)
    given = swap(jnp.concatenate([n1_given, x_given], axis=1), "zh")
    n1_own = jnp.concatenate([pick(n1_own, given), pick(given, n1_own)], axis=0)

    column = exchange(jnp.concatenate([jnp.tile(second[1], (4, 1)), jnp.tile(second[0], (4, 1))], axis=0), ("zh", "zl"))
    block = [column] + [lax.ppermute(column, "x", [(i, i ^ step) for i in range(4)]) for step in (1, 2, 3)]
    block = jnp.concatenate(block, axis=0)
    n1 = exchange(jnp.tile(n1_own, (8, 1)), "y")
    terms = grad_terms(n1, [block, swap(block, "core")])

    features = n1[:, E + LANES :]
    chunk = E // 8
    half = chunk // 2
    terms, features, core = lax.optimization_barrier((terms, features, lax.axis_index("core")))
    parts, features, core = lax.optimization_barrier((exchange(terms, "y"), features, core))
    dpre = jnp.sum(parts.astype(f32).reshape(8, chunk, -1), axis=0).astype(bf16)
    kept = jnp.where(core == 0, dpre[:half], dpre[half:])
    given = jnp.where(core == 0, dpre[half:], dpre[:half])
    given = swap(jnp.dot(given, features, preferred_element_type=f32).astype(bf16), "core")
    weight_grad = jnp.dot(kept, features, preferred_element_type=f32) + given.astype(f32)
    parts = weight_grad.astype(bf16).reshape(half, 16, LANES).transpose(1, 0, 2).reshape(16 * half, LANES)
    parts = exchange(parts, TXT).astype(f32).reshape(16, half, LANES)
    weight_grad = jnp.sum(parts, axis=0).astype(bf16)
    halves = exchange(jnp.tile(weight_grad, (16, 1)), ZY)
    whole = lax.all_gather(halves, "core", axis=0, tiled=False).reshape(2, 16, half, LANES).astype(f32)
    whole = whole.transpose(1, 0, 2, 3).reshape(2 * E, LANES)
    return whole[:E, :image_cols].T, whole[E:, :text_cols].T


def solution(mesh):
    fine = Mesh(mesh.devices.reshape(2, 8, 2, 4, 4), AXES)
    in_specs = (P(IMG, TXT), P(IMG, TXT), P(TXT, None), P(TXT, None), P(IMG))
    out_specs = (P(TXT, None), P(TXT, None))
    return jax.shard_map(local, mesh=fine, in_specs=in_specs, out_specs=out_specs, check_vma=False)
```

```python
import jax
import jax.numpy as jnp
from jax import lax
from jax.experimental import pallas as pl
from jax.sharding import Mesh
from jax.sharding import PartitionSpec as P

LOGIT_SCALE = 10.0
LOGIT_BIAS = -5.0
EPS = 1e-06
E = 1152
LANES = 128
SPARE = 96
AXES = ("zh", "y", "core", "zl", "x")
IMG = ("zh", "y", "core")
ZY = ("zh", "y")
TXT = ("zl", "x")
bf16 = jnp.bfloat16
f32 = jnp.float32


def exchange(value, axis):
    return lax.all_to_all(value, axis, 0, 0, tiled=True)


def swap(value, axis):
    return lax.ppermute(value, axis, [(0, 1), (1, 0)])


def head_kernel(image_ref, text_ref, image_weight_ref, text_weight_ref, out_ref):
    tn = (((0,), (0,)), ((), ()))
    for tower, (features, weight) in enumerate(((image_ref, image_weight_ref), (text_ref, text_weight_ref))):
        rows = features[...]
        out_ref[:, tower * E : (tower + 1) * E] = lax.dot_general(
            rows, weight[...], tn, preferred_element_type=f32
        ).astype(bf16)
        square = (rows.shape[0], LANES)
        same = lax.broadcasted_iota(jnp.int32, square, 0) == lax.broadcasted_iota(jnp.int32, square, 1)
        place = jnp.where(same, 1.0, 0.0).astype(bf16)
        out_ref[:, 2 * E + tower * LANES : 2 * E + (tower + 1) * LANES] = lax.dot_general(
            rows, place, tn, preferred_element_type=f32
        ).astype(bf16)


def head_partials(image_features, text_features, image_weight, text_weight):
    return pl.pallas_call(
        head_kernel,
        out_shape=jax.ShapeDtypeStruct((image_features.shape[0], 2 * E + 2 * LANES), bf16),
        name="head_partials",
    )(image_features.T, text_features.T, image_weight, text_weight)


def columns_in_lanes(columns, rows, first=0):
    lane = lax.broadcasted_iota(jnp.int32, (rows, LANES), 1)
    lanes = jnp.zeros((rows, LANES), f32)
    for place, column in enumerate(columns):
        lanes = jnp.where(lane == first + place, column, lanes)
    return lanes


def key_digits(key):
    hi = jnp.floor(key * (1.0 / 64.0))
    return [hi, key - 64.0 * hi]


def hi_lo(value):
    hi = value.astype(bf16).astype(f32)
    return [hi, value - hi]


def unit_rows(partials, pairs, ids):
    rows = partials.shape[0] // 16
    total = jnp.sum(partials[:, : 2 * E].astype(f32).reshape(16, rows, 2 * E), axis=0)
    first, second = [], []
    for tower, (key1, key2) in enumerate(((pairs, pairs), (ids, ids))):
        pre = total[:, tower * E : (tower + 1) * E]
        scale = lax.rsqrt(jnp.sum(pre * pre, -1, keepdims=True) + EPS)
        unit = pre * scale
        extra1 = columns_in_lanes(key_digits(key1) + hi_lo(scale), rows, SPARE)
        extra2 = columns_in_lanes(key_digits(key2), rows)
        first.append((unit.astype(bf16), extra1.astype(bf16)))
        second.append(jnp.concatenate([unit, extra2], axis=1).astype(bf16))
    return first, second


def grad_terms(n1, n2_blocks):
    rows = n1.shape[0]
    info = n1[:, E : E + LANES].astype(f32)
    key1 = info[:, SPARE : SPARE + 1] * 64.0 + info[:, SPARE + 1 : SPARE + 2]
    scale = info[:, SPARE + 2 : SPARE + 3] + info[:, SPARE + 3 : SPARE + 4]
    unit = n1[:, :E]
    grad = jnp.zeros((rows, E), f32)
    for block in n2_blocks:
        other = block[:, :E]
        info2 = block[:, E:].astype(f32).T
        key2 = info2[0:1] * 64.0 + info2[1:2]
        scores = lax.dot_general(unit, other, (((1,), (1,)), ((), ())), preferred_element_type=f32)
        logits = LOGIT_SCALE * scores + LOGIT_BIAS
        label = jnp.where(key1 == key2, 1.0, 0.0)
        pair_grad = (1.0 / (1.0 + jnp.exp(-logits)) - label).astype(bf16)
        grad = grad + jnp.dot(pair_grad, other, preferred_element_type=f32)
    unit = unit.astype(f32)
    along = jnp.sum(unit * grad, -1, keepdims=True)
    return ((grad - unit * along) * (scale * LOGIT_SCALE)).T.astype(bf16)


def local(image_features, text_features, image_weight, text_weight, pair_index):
    zh = lax.axis_index("zh")
    img = lax.axis_index(IMG)
    txt = lax.axis_index(TXT)
    block_rows = image_features.shape[0]
    own_rows = block_rows // 16
    image_cols = image_features.shape[1]
    text_cols = text_features.shape[1]

    def pick(one, two):
        return jnp.where(zh == 0, one, two)

    partials = exchange(head_partials(image_features, text_features, image_weight, text_weight), TXT)

    def all_features(tower):
        part = partials[:, 2 * E + tower * LANES : 2 * E + (tower + 1) * LANES]
        return part.reshape(16, own_rows, LANES).transpose(1, 0, 2).reshape(own_rows, 16 * LANES)

    pairs = lax.dynamic_slice_in_dim(pair_index, txt * own_rows, own_rows, 0).astype(f32)[:, None]
    ids = (img * block_rows + txt * own_rows + jnp.arange(own_rows)).astype(f32)[:, None]
    first, second = unit_rows(partials, pairs, ids)
    for tower, (unit, extra) in enumerate(first):
        lanes = all_features(tower)
        first[tower] = jnp.concatenate([unit, lanes[:, :LANES] + extra, lanes[:, LANES:]], axis=1)

    n1_own, n1_given = pick(*first), pick(*first[::-1])
    given = swap(n1_given, "zh")
    n1_own = jnp.concatenate([pick(n1_own, given), pick(given, n1_own)], axis=0)

    column = exchange(jnp.concatenate([jnp.tile(second[1], (4, 1)), jnp.tile(second[0], (4, 1))], axis=0), ("zh", "zl"))
    block = [column] + [lax.ppermute(column, "x", [(i, i ^ step) for i in range(4)]) for step in (1, 2, 3)]
    block = jnp.concatenate(block, axis=0)
    n1 = exchange(jnp.tile(n1_own, (8, 1)), "y")
    terms = grad_terms(n1, [block, swap(block, "core")])

    features = n1[:, E:]
    chunk = E // 8
    half = chunk // 2
    terms, features, core = lax.optimization_barrier((terms, features, lax.axis_index("core")))
    parts, features, core = lax.optimization_barrier((exchange(terms, "y"), features, core))
    dpre = jnp.sum(parts.astype(f32).reshape(8, chunk, -1), axis=0).astype(bf16)
    kept = jnp.where(core == 0, dpre[:half], dpre[half:])
    given = jnp.where(core == 0, dpre[half:], dpre[:half])
    given = swap(jnp.dot(given, features, preferred_element_type=f32).astype(bf16), "core")
    weight_grad = jnp.dot(kept, features, preferred_element_type=f32) + given.astype(f32)
    parts = weight_grad.astype(bf16).reshape(half, 16, LANES).transpose(1, 0, 2).reshape(16 * half, LANES)
    parts = exchange(parts, TXT).astype(f32).reshape(16, half, LANES)
    weight_grad = jnp.sum(parts, axis=0).astype(bf16)
    halves = exchange(jnp.tile(weight_grad, (16, 1)), ZY)
    whole = lax.all_gather(halves, "core", axis=0, tiled=False).reshape(2, 16, half, LANES).astype(f32)
    whole = whole.transpose(1, 0, 2, 3).reshape(2 * E, LANES)
    return whole[:E, :image_cols].T, whole[E:, :text_cols].T


def solution(mesh):
    fine = Mesh(mesh.devices.reshape(2, 8, 2, 4, 4), AXES)
    in_specs = (P(IMG, TXT), P(IMG, TXT), P(TXT, None), P(TXT, None), P(IMG))
    out_specs = (P(TXT, None), P(TXT, None))
    return jax.shard_map(local, mesh=fine, in_specs=in_specs, out_specs=out_specs, check_vma=False)
```
